32 devices in a mesh: group: 2 (over y), blk: 4 (over z), head: 4 (over x, core).
Axes of the slice: x: 2, y: 2, z: 4, core: 2. Of those that a mesh axis runs over, the one named last changes fastest.
Arguments:
- query_a: bfloat16 [768, 5120], P(('group', 'blk', 'head')), parts along dimension 0, may hold values from -600 to 600
- key_a: bfloat16 [768, 5120], P(('group', 'blk', 'head')), parts along dimension 0, may hold values from -600 to 600
- value_a: bfloat16 [768, 5120], P(('group', 'blk', 'head')), parts along dimension 0, may hold values from -6 to 6
- query_b: bfloat16 [768, 5120], P(('group', 'blk', 'head')), parts along dimension 0, may hold values from -600 to 600
- key_b: bfloat16 [768, 5120], P(('group', 'blk', 'head')), parts along dimension 0, may hold values from -600 to 600
- value_b: bfloat16 [768, 5120], P(('group', 'blk', 'head')), parts along dimension 0, may hold values from -6 to 6
- query_gain: float32 [5120], replicated, may hold values from 0.8 to 2.5
- key_gain: float32 [5120], replicated, may hold values from 0.8 to 2.5
Outputs:
- attended_a: bfloat16 [768, 5120], P(('group', 'blk', 'head')), parts along dimension 0
- attended_b: bfloat16 [768, 5120], P(('group', 'blk', 'head')), parts along dimension 0
The draws below stay inside these ranges and needn't reach their ends.
There are 2 independent parts, one for each index of `group`. The reference program is written for one: setup_inputs(seed, part) draws one part's arguments, and reference() takes and returns one part's arrays. A program takes and returns all parts, laid end to end along the dimension named above; an argument that names none is the same for every part. Nothing has to cross between parts.
All inputs are finite; a program needn't handle non-finite values. Where the reference program divides by a largest or mean magnitude, that divisor is 1e-20 or more.
Results may differ from the reference program's by a relative error of at most 0.001.
The reference program's roundings to bfloat16 on the way count: a program that leaves them out, or rounds other values in their place, can miss the bound.
Values may be sent and summed in bfloat16 or wider, within the bound.
A program may use at most 64 MiB of HBM per device.

```python
import math
import jax
import jax.numpy as jnp
from jax import lax

D = 5120
HEADS = 40
HEAD_DIM = 128
TOKENS = 384


def common_parts(key, spike_level):
    col_scale = jnp.exp(jax.random.uniform(jax.random.fold_in(key, 41), (1, D), jnp.float32, 0.0, math.log(10.0)))
    row_scale = jnp.exp(jax.random.uniform(jax.random.fold_in(key, 42), (TOKENS, 1), jnp.float32, 0.0, math.log(10.0)))
    pair_count = 8
    query_rows = jax.random.randint(jax.random.fold_in(key, 43), (pair_count,), 0, TOKENS)
    key_rows = jax.random.randint(jax.random.fold_in(key, 44), (pair_count,), 0, TOKENS)
    twin_rows = jax.random.randint(jax.random.fold_in(key, 45), (pair_count,), 0, TOKENS)
    head_pick = jax.random.randint(jax.random.fold_in(key, 46), (pair_count,), 0, HEADS)
    direction = jax.random.truncated_normal(jax.random.fold_in(key, 47), -3.0, 3.0, (pair_count, HEAD_DIM), jnp.float32)
    strength = 40.0 + 40.0 * jnp.arange(pair_count, dtype=jnp.float32) / (pair_count - 1)
    jitter = 1.0 + 0.05 * jax.random.truncated_normal(jax.random.fold_in(key, 48), -3.0, 3.0, (pair_count, D), jnp.float32)
    key_noise = jax.random.truncated_normal(jax.random.fold_in(key, 49), -4.0, 4.0, (TOKENS, D), jnp.float32)
    positions = jnp.arange(TOKENS)
    head_cols = jnp.arange(D) // HEAD_DIM
    in_head = (head_cols[None, :] == head_pick[:, None]).astype(jnp.float32)
    pattern = jnp.tile(direction, (1, HEADS)) * in_head * strength[:, None] * spike_level
    hit_query = (positions[:, None] == query_rows[None, :]).astype(jnp.float32)
    hit_key = (positions[:, None] == key_rows[None, :]).astype(jnp.float32)
    hit_twin = (positions[:, None] == twin_rows[None, :]).astype(jnp.float32)
    query_spike = jnp.dot(hit_query, pattern, precision=lax.Precision.HIGHEST)
    key_spike = jnp.dot(hit_key, pattern, precision=lax.Precision.HIGHEST) + jnp.dot(hit_twin, pattern * jitter, precision=lax.Precision.HIGHEST)
    query_scale = col_scale * row_scale
    key_scale = col_scale * row_scale
    return (query_spike, key_spike, query_scale, key_scale, key_noise)


def draw_query_a(key, part):
    spike_level = 0.0
    query_spike, key_spike, query_scale, key_scale, key_noise = common_parts(key, spike_level)
    key = jax.random.fold_in(key, 1)
    own_noise = jax.random.truncated_normal(key, -4.0, 4.0, (TOKENS, D), jnp.float32)
    return (own_noise * query_scale + query_spike).astype(jnp.bfloat16)


def draw_query_b(key, part):
    spike_level = 0.0
    query_spike, key_spike, query_scale, key_scale, key_noise = common_parts(key, spike_level)
    key = jax.random.fold_in(key, 2)
    own_noise = jax.random.truncated_normal(key, -4.0, 4.0, (TOKENS, D), jnp.float32)
    return (own_noise * query_scale + query_spike).astype(jnp.bfloat16)


def draw_key_a(key, part):
    spike_level = 0.0
    query_spike, key_spike, query_scale, key_scale, key_noise = common_parts(key, spike_level)
    return (key_noise * key_scale + key_spike).astype(jnp.bfloat16)


def draw_key_b(key, part):
    spike_level = 0.0
    query_spike, key_spike, query_scale, key_scale, key_noise = common_parts(key, spike_level)
    key = jax.random.fold_in(key, 4)
    own_noise = jax.random.truncated_normal(key, -4.0, 4.0, (TOKENS, D), jnp.float32)
    return ((0.9 * key_noise + 0.45 * own_noise) * key_scale + key_spike).astype(jnp.bfloat16)


def block_levels(key, shape, shards, smallest, top_value):
    loudness, own = 1.0, jax.random.fold_in(key, 6)
    for dim, shards_of in shards:
        heights = jnp.exp(jax.random.uniform(jax.random.fold_in(own, dim), (shards_of,), jnp.float32, smallest / len(shards), top_value / len(shards)))
        loudness = loudness * jnp.repeat(heights, shape[dim] // shards_of).reshape([-1 if axis == dim else 1 for axis in range(len(shape))])
    return loudness


def gaussian(key, dims, scale, bound, pieces=(), kind=jnp.bfloat16):
    factor_of = block_levels(key, dims, pieces, -0.22, 0.18) if pieces else 1.0
    drawn = jax.random.normal(key, dims, jnp.float32) * scale * factor_of
    return jnp.minimum(jnp.maximum(drawn, -bound), bound).astype(kind)


def setup_inputs(seed: int = 0, part: int = 0) -> dict:
    seeds = jax.random.split(jax.random.key(seed), 9)
    part_splits = jax.random.split(jax.random.fold_in(seeds[8], part), 9)
    return {
        "query_a": draw_query_a(jax.random.fold_in(jax.random.fold_in(seeds[8], part), 71), part),
        "key_a": draw_key_a(jax.random.fold_in(jax.random.fold_in(seeds[8], part), 71), part),
        "value_a": gaussian(part_splits[2], (TOKENS, D), 1.0, 6.0, ((0, 16),)),
        "query_b": draw_query_b(jax.random.fold_in(jax.random.fold_in(seeds[8], part), 71), part),
        "key_b": draw_key_b(jax.random.fold_in(jax.random.fold_in(seeds[8], part), 71), part),
        "value_b": gaussian(part_splits[5], (TOKENS, D), 1.0, 6.0, ((0, 16),)),
        "query_gain": jnp.clip(jnp.exp(jax.random.uniform(seeds[6], (D,), jnp.float32, math.log(0.8), math.log(2.5))), 0.8, 2.5),
        "key_gain": jnp.clip(jnp.exp(jax.random.uniform(seeds[7], (D,), jnp.float32, math.log(0.8), math.log(2.5))), 0.8, 2.5),
    }


norm_eps = 1e-06

def normalize(values, gain_vec):
    widened = values.astype(jnp.float32)
    inverse = lax.rsqrt(lax.optimization_barrier(jnp.mean(widened * widened, axis=-1, keepdims=True)) + norm_eps)
    return (widened * inverse * gain_vec).astype(jnp.bfloat16)

def by_heads(matrix):
    return jnp.transpose(matrix.reshape(TOKENS, HEADS, HEAD_DIM), (1, 0, 2))

def binary_scale(magnitude):
    factor_now = jnp.full(magnitude.shape, 2.0 ** (-20), jnp.float32)
    for exponent in range(-20, 10):
        factor_now = factor_now * jnp.where(magnitude >= 2.0 ** exponent, 2.0, 1.0)
    return factor_now

def coarse_code(ratio):
    step_size = jnp.full(ratio.shape, 2.0 ** (-17), jnp.float32)
    magnitude = jnp.abs(ratio)
    for exponent in range(1, 15):
        step_size = step_size * jnp.where(magnitude >= 2.0 ** (-exponent), 2.0, 1.0)
    return jnp.floor(ratio / step_size + 0.5) * step_size

def rough_head(operands):
    queries, key_rows, values = operands
    scores = jnp.dot(queries, key_rows.T, preferred_element_type=jnp.float32) * (1.0 / math.sqrt(HEAD_DIM))
    weights = jnp.exp(scores - lax.optimization_barrier(jnp.max(scores, axis=1, keepdims=True)))
    denominator = lax.optimization_barrier(jnp.sum(weights, axis=1, keepdims=True))
    return jnp.dot(weights.astype(jnp.bfloat16), values, preferred_element_type=jnp.float32) / denominator

def exact_head(operands):
    queries, key_rows, values = operands
    scores = jnp.dot(queries, key_rows.T, precision=lax.Precision.HIGHEST) * (1.0 / math.sqrt(HEAD_DIM))
    weights = jnp.exp(scores - lax.optimization_barrier(jnp.max(scores, axis=1, keepdims=True)))
    denominator = lax.optimization_barrier(jnp.sum(weights, axis=1, keepdims=True))
    return jnp.dot(weights, values, precision=lax.Precision.HIGHEST) / denominator

def rebuild(cached, fresh_rows):
    shaped_old = cached.astype(jnp.float32).reshape(TOKENS, HEADS, HEAD_DIM)
    residual = fresh_rows.astype(jnp.float32).reshape(TOKENS, HEADS, HEAD_DIM) - shaped_old
    block_scale = binary_scale(lax.optimization_barrier(jnp.max(jnp.abs(residual), axis=-1, keepdims=True))).astype(jnp.bfloat16)
    code_rows = coarse_code(residual / block_scale.astype(jnp.float32)).astype(jnp.bfloat16)
    rebuilt = shaped_old + block_scale.astype(jnp.float32) * code_rows.astype(jnp.float32)
    return rebuilt.reshape(TOKENS, D)

def reference(query_a, key_a, value_a, query_b, key_b, value_b, query_gain, key_gain):
    normed_qa = normalize(query_a, query_gain)
    normed_ka = normalize(key_a, key_gain)
    normed_qb = normalize(query_b, query_gain)
    normed_kb = normalize(key_b, key_gain)
    first_out = lax.map(rough_head, (by_heads(normed_qa), by_heads(normed_ka), by_heads(value_a)))
    attended_a = jnp.transpose(first_out, (1, 0, 2)).reshape(TOKENS, D).astype(jnp.bfloat16)
    rebuilt_keys = rebuild(normed_ka, normed_kb)
    rebuilt_values = rebuild(value_a, value_b)
    second = lax.map(exact_head, (by_heads(normed_qb).astype(jnp.float32), by_heads(rebuilt_keys), by_heads(rebuilt_values)))
    attended_b = jnp.transpose(second, (1, 0, 2)).reshape(TOKENS, D).astype(jnp.bfloat16)
    return (attended_a, attended_b)
```

```python
import functools
import math

import jax
import jax.numpy as jnp
from jax import lax
from jax.experimental import pallas as pl
from jax.experimental.pallas import tpu as pltpu
from jax.sharding import PartitionSpec as P

HEADS = 40
HEAD_DIM = 128


norm_eps = 1e-06


def normalize(values, gain_vec):
    widened = values.astype(jnp.float32)
    inverse = lax.rsqrt(jnp.mean(widened * widened, axis=-1, keepdims=True) + norm_eps)
    return (widened * inverse * gain_vec).astype(jnp.bfloat16)


def to_heads(matrix):
    return matrix.reshape(matrix.shape[0], HEADS, HEAD_DIM)


def binary_scale(magnitude):
    factor_now = jnp.full(magnitude.shape, 2.0 ** (-20), jnp.float32)
    for exponent in range(-20, 10):
        factor_now = factor_now * jnp.where(magnitude >= 2.0**exponent, 2.0, 1.0)
    return factor_now


def coarse_code(ratio):
    step_size = jnp.full(ratio.shape, 2.0 ** (-17), jnp.float32)
    magnitude = jnp.abs(ratio)
    for exponent in range(1, 15):
        step_size = step_size * jnp.where(magnitude >= 2.0 ** (-exponent), 2.0, 1.0)
    return jnp.floor(ratio / step_size + 0.5) * step_size


def block_length(total_rows):
    return max(
        (step_len for step_len in range(1, min(total_rows, 512) + 1) if total_rows % step_len == 0)
    )


def absorb(status, scores, value_rows, precise):
    run_max, run_sum, run_acc = status
    new_max = jnp.maximum(run_max, jnp.max(scores, axis=-1))
    factor = jnp.exp(run_max - new_max)
    weights = jnp.exp(scores - new_max[..., None])
    run_sum = run_sum * factor + jnp.sum(weights, axis=-1)
    if precise:
        update = jnp.einsum("qhk,khd->qhd", weights, value_rows, precision=lax.Precision.HIGHEST)
    else:
        update = jnp.einsum(
            "qhk,khd->qhd",
            weights.astype(jnp.bfloat16),
            value_rows,
            preferred_element_type=jnp.float32,
        )
    return (new_max, run_sum, run_acc * factor[..., None] + update)


def sweep(status, total_rows, block_fn):
    length = block_length(total_rows)

    def one_block(block_no, current):
        return block_fn(current, block_no * length, length)

    return lax.fori_loop(0, total_rows // length, one_block, status)


def rough_blocks(queries, key_rows, value_rows):
    inv_root = 1.0 / math.sqrt(queries.shape[-1])

    def block_fn(current, offset, length):
        key_blk = lax.dynamic_slice_in_dim(key_rows, offset, length, 0)
        value_blk = lax.dynamic_slice_in_dim(value_rows, offset, length, 0)
        scores = (
            jnp.einsum("qhd,khd->qhk", queries, key_blk, preferred_element_type=jnp.float32)
            * inv_root
        )
        return absorb(current, scores, value_blk, False)

    return block_fn


def exact_blocks(queries, cache_keys, cache_values, coded_rows, row_base):
    code_keys, code_values, scale_keys, scale_values = coded_rows
    inv_root = 1.0 / math.sqrt(queries.shape[-1])

    def block_fn(current, offset, length):
        old_keys = lax.dynamic_slice_in_dim(cache_keys, row_base + offset, length, 0).astype(
            jnp.float32
        )
        old_values = lax.dynamic_slice_in_dim(cache_values, row_base + offset, length, 0).astype(
            jnp.float32
        )
        key_scale = lax.dynamic_slice_in_dim(scale_keys, offset, length, 0).astype(jnp.float32)
        value_scale = lax.dynamic_slice_in_dim(scale_values, offset, length, 0).astype(jnp.float32)
        new_keys = old_keys + key_scale[..., None] * lax.dynamic_slice_in_dim(
            code_keys, offset, length, 0
        ).astype(jnp.float32)
        new_values = old_values + value_scale[..., None] * lax.dynamic_slice_in_dim(
            code_values, offset, length, 0
        ).astype(jnp.float32)
        scores = (
            jnp.einsum("qhd,khd->qhk", queries, new_keys, precision=lax.Precision.HIGHEST)
            * inv_root
        )
        return absorb(current, scores, new_values, True)

    return block_fn


def fresh_status(queries):
    leading = queries.shape[:2]
    return (
        jnp.full(leading, -jnp.inf, jnp.float32),
        jnp.zeros(leading, jnp.float32),
        jnp.zeros(queries.shape, jnp.float32),
    )


def finish(status):
    run_max, run_sum, run_acc = status
    return (run_acc / run_sum[..., None]).astype(jnp.bfloat16)


def send_back(result):
    moved = lax.all_to_all(result, "head", split_axis=0, concat_axis=1, tiled=True)
    return moved.reshape(moved.shape[0], moved.shape[1] * moved.shape[2])


def prepare(query, key_rows, value_rows, query_gain, key_gain):
    moved_query, moved_key, moved_value = (
        lax.all_to_all(
            to_heads(normalize(query, query_gain)), "head", split_axis=1, concat_axis=0, tiled=True
        ),
        lax.all_to_all(
            to_heads(normalize(key_rows, key_gain)), "head", split_axis=1, concat_axis=0, tiled=True
        ),
        lax.all_to_all(to_heads(value_rows), "head", split_axis=1, concat_axis=0, tiled=True),
    )
    return (moved_query, moved_key, moved_value)


def shards(query_a, key_a, value_a, query_b, key_b, value_b, query_gain, key_gain):
    queries_a, keys_a, values_a = prepare(query_a, key_a, value_a, query_gain, key_gain)
    queries_b, keys_b, values_b = prepare(query_b, key_b, value_b, query_gain, key_gain)
    total_rows = keys_a.shape[0] * lax.axis_size("blk")
    start_a = fresh_status(queries_a)
    cache_keys, cache_values = (
        lax.all_gather(keys_a, "blk", axis=0, tiled=True),
        lax.all_gather(values_a, "blk", axis=0, tiled=True),
    )
    status_a = sweep(start_a, total_rows, rough_blocks(queries_a, cache_keys, cache_values))
    attended_a = send_back(finish(status_a))
    residual_key = keys_b.astype(jnp.float32) - keys_a.astype(jnp.float32)
    residual_value = values_b.astype(jnp.float32) - values_a.astype(jnp.float32)
    scale_key = binary_scale(jnp.max(jnp.abs(residual_key), axis=-1)).astype(jnp.bfloat16)
    scale_value = binary_scale(jnp.max(jnp.abs(residual_value), axis=-1)).astype(jnp.bfloat16)
    code_key = coarse_code(residual_key / scale_key.astype(jnp.float32)[..., None]).astype(
        jnp.bfloat16
    )
    code_value = coarse_code(residual_value / scale_value.astype(jnp.float32)[..., None]).astype(
        jnp.bfloat16
    )
    queries_wide = queries_b.astype(jnp.float32)
    start_b = fresh_status(queries_b)
    gathered = (
        lax.all_gather(code_key, "blk", axis=0, tiled=True),
        lax.all_gather(code_value, "blk", axis=0, tiled=True),
        lax.all_gather(scale_key, "blk", axis=0, tiled=True),
        lax.all_gather(scale_value, "blk", axis=0, tiled=True),
    )
    status_b = sweep(
        start_b, total_rows, exact_blocks(queries_wide, cache_keys, cache_values, gathered, 0)
    )
    attended_b = send_back(finish(status_b))
    return (attended_a, attended_b)


MESH = pl.DeviceIdType.MESH


def stepped_code(ratio):
    magnitude = jnp.abs(ratio)
    step_size = jnp.full(ratio.shape, 2.0 ** (-17), jnp.float32)
    inverse = jnp.full(ratio.shape, 2.0**17, jnp.float32)
    for exponent in range(14, 0, -1):
        reached = magnitude >= 2.0 ** (-exponent)
        step_size = jnp.where(reached, 2.0 ** (-2 - exponent), step_size)
        inverse = jnp.where(reached, 2.0 ** (2 + exponent), inverse)
    return jnp.floor(ratio * inverse + 0.5) * step_size


def coded_residual(fresh, cached):
    residual = fresh - cached
    magnitude = jnp.max(jnp.abs(residual), axis=-1, keepdims=True)
    scale = jnp.full(magnitude.shape, 2.0 ** (-20), jnp.float32)
    inverse = jnp.full(magnitude.shape, 2.0**20, jnp.float32)
    for exponent in range(-20, 10):
        reached = magnitude >= 2.0**exponent
        scale = jnp.where(reached, 2.0 ** (exponent + 1), scale)
        inverse = jnp.where(reached, 2.0 ** (-exponent - 1), inverse)
    return stepped_code(residual * inverse) * scale


def fused_kernel(
    sizes, qa, ka, va, qb, kb, vb, q_gain, k_gain, out_a, out_b,
    send_a, send_b, got_a, got_b, twin_a, twin_b, back_a, back_b,
    ssem, rsem, tsem, usem, osem, psem,
):
    blks, lanes, own_heads = sizes
    half_lanes = lanes // 2
    peers = blks * half_lanes
    rows, width = qa.shape
    span = own_heads * HEAD_DIM
    blk, lane = lax.axis_index("blk"), lax.axis_index("head")
    side, core = lane // 2, lane % 2
    me = blk * half_lanes + side
    here = {"group": lax.axis_index("group")}

    def place(peer):
        return {**here, "blk": peer // half_lanes, "head": (peer % half_lanes) * 2 + core}

    twin = {**here, "blk": blk, "head": side * 2 + 1 - core}

    def target(i):
        return (me + i + 1) % peers

    def source(i):
        return (me + 2 * peers - 1 - i) % peers

    barrier = pltpu.get_barrier_semaphore()

    @pl.loop(0, peers - 1)
    def _(i):
        pl.semaphore_signal(barrier, inc=1, device_id=place(target(i)), device_id_type=MESH)

    pl.semaphore_signal(barrier, inc=1, device_id=twin, device_id_type=MESH)

    def columns(start):
        return pl.ds(pl.multiple_of(start, HEAD_DIM), HEAD_DIM)

    def inverse_norm(ref):
        def add(h, total):
            piece = ref[:, columns(h * HEAD_DIM)].astype(jnp.float32)
            return total + piece * piece

        total = lax.fori_loop(
            0, width // HEAD_DIM, add, jnp.zeros((rows, HEAD_DIM), jnp.float32), unroll=8
        )
        mean = jnp.sum(total, axis=-1, keepdims=True) * (1.0 / width)
        return lax.rsqrt(mean + norm_eps)

    inv_qa, inv_ka = inverse_norm(qa), inverse_norm(ka)
    inv_qb, inv_kb = inverse_norm(qb), inverse_norm(kb)
    pl.semaphore_wait(barrier, peers)

    def normed(ref, inverse, gain, cols):
        piece = ref[:, cols].astype(jnp.float32)
        return (piece * inverse * gain[:, cols]).astype(jnp.bfloat16)

    def fill_a(dest, slot, peer):
        for h in range(own_heads):
            cols, local = columns(peer * span + h * HEAD_DIM), pl.ds(h * HEAD_DIM, HEAD_DIM)
            dest[slot, 0, :, local] = normed(qa, inv_qa, q_gain, cols)
            dest[slot, 1, :, local] = normed(ka, inv_ka, k_gain, cols)
            dest[slot, 2, :, local] = va[:, cols]

    def fill_b(dest, slot, peer):
        for h in range(own_heads):
            cols, local = columns(peer * span + h * HEAD_DIM), pl.ds(h * HEAD_DIM, HEAD_DIM)
            dest[slot, 0, :, local] = normed(qb, inv_qb, q_gain, cols)
            fresh = normed(kb, inv_kb, k_gain, cols).astype(jnp.float32)
            cached = normed(ka, inv_ka, k_gain, cols).astype(jnp.float32)
            dest[slot, 1, :, local] = coded_residual(fresh, cached).astype(jnp.bfloat16)
            dest[slot, 2, :, local] = coded_residual(
                vb[:, cols].astype(jnp.float32), va[:, cols].astype(jnp.float32)
            ).astype(jnp.bfloat16)

    def forth(step, send, got, peer, slot):
        return pltpu.make_async_remote_copy(
            src_ref=send.at[peer],
            dst_ref=got.at[slot],
            send_sem=ssem.at[step, peer],
            recv_sem=rsem.at[step, slot],
            device_id=place(peer),
            device_id_type=MESH,
        )

    def across(step, got, other, slot):
        return pltpu.make_async_remote_copy(
            src_ref=got.at[slot, pl.ds(1, 2)],
            dst_ref=other.at[slot],
            send_sem=tsem.at[step, slot],
            recv_sem=usem.at[step, slot],
            device_id=twin,
            device_id_type=MESH,
        )

    def home(step, back, out, peer, slot):
        return pltpu.make_async_remote_copy(
            src_ref=back.at[peer],
            dst_ref=out.at[slot],
            send_sem=osem.at[step, peer],
            recv_sem=psem.at[step, slot],
            device_id=place(peer),
            device_id_type=MESH,
        )

    @pl.loop(0, peers - 1)
    def _(i):
        peer = target(i)
        fill_a(send_a, peer, peer)
        forth(0, send_a, got_a, peer, me).start()

    fill_a(got_a, me, me)
    across(0, got_a, twin_a, me).start()

    @pl.loop(0, peers - 1)
    def _(i):
        peer = target(i)
        fill_b(send_b, peer, peer)
        forth(1, send_b, got_b, peer, me).start()

    fill_b(got_b, me, me)
    across(1, got_b, twin_b, me).start()

    inv_root = 1.0 / math.sqrt(HEAD_DIM)

    def collect(step, send, got, other):
        @pl.loop(0, peers - 1)
        def _(i):
            slot = source(i)
            forth(step, send, got, slot, slot).wait_recv()
            across(step, got, other, slot).start()

        @pl.loop(0, peers)
        def _(slot):
            across(step, got, other, slot).wait_recv()

    def gather_rows(got, other, part, cols):
        own = got[:, part, :, cols].astype(jnp.float32).reshape(peers * rows, HEAD_DIM)
        far = other[:, part - 1, :, cols].astype(jnp.float32).reshape(peers * rows, HEAD_DIM)
        return jnp.concatenate([own, far], axis=0).astype(jnp.bfloat16)

    def query_rows(got, cols):
        own = got[:, 0, :, cols].astype(jnp.float32).reshape(peers * rows, HEAD_DIM)
        return own.astype(jnp.bfloat16)

    def scores_of(queries, keys):
        return (
            lax.dot_general(
                queries, keys, (((1,), (1,)), ((), ())), preferred_element_type=jnp.float32
            )
            * inv_root
        )

    def store_head(back, cols, result):
        back[:, :, cols] = result.reshape(peers, rows, HEAD_DIM).astype(jnp.bfloat16)

    def send_home(step, back, out):
        @pl.loop(0, peers - 1)
        def _(i):
            home(step, back, out, target(i), me).start()

        out[me] = back[me]

    collect(0, send_a, got_a, twin_a)

    @pl.loop(0, own_heads)
    def _(h):
        cols = columns(h * HEAD_DIM)
        scores = scores_of(query_rows(got_a, cols), gather_rows(got_a, twin_a, 1, cols))
        weights = jnp.exp(scores - jnp.max(scores, axis=1, keepdims=True))
        total = jnp.sum(weights, axis=1, keepdims=True)
        values = gather_rows(got_a, twin_a, 2, cols)
        mixed = jnp.dot(weights.astype(jnp.bfloat16), values, preferred_element_type=jnp.float32)
        store_head(back_a, cols, mixed / total)

    send_home(0, back_a, out_a)
    collect(1, send_b, got_b, twin_b)

    @pl.loop(0, own_heads)
    def _(h):
        cols = columns(h * HEAD_DIM)
        queries = query_rows(got_b, cols)
        keys = jnp.concatenate(
            [gather_rows(got_a, twin_a, 1, cols), gather_rows(got_b, twin_b, 1, cols)], axis=1
        )
        scores = scores_of(jnp.concatenate([queries, queries], axis=1), keys)
        weights = jnp.exp(scores - jnp.max(scores, axis=1, keepdims=True))
        total = jnp.sum(weights, axis=1, keepdims=True)
        values = jnp.concatenate(
            [gather_rows(got_a, twin_a, 2, cols), gather_rows(got_b, twin_b, 2, cols)], axis=1
        )
        coarse = weights.astype(jnp.bfloat16)
        fine = (weights - coarse.astype(jnp.float32)).astype(jnp.bfloat16)
        mixed = jnp.dot(coarse, values, preferred_element_type=jnp.float32) + jnp.dot(
            fine, values, preferred_element_type=jnp.float32
        )
        store_head(back_b, cols, (mixed[:, :HEAD_DIM] + mixed[:, HEAD_DIM:]) / total)

    send_home(1, back_b, out_b)

    for step, send, got, other, back, out in (
        (0, send_a, got_a, twin_a, back_a, out_a),
        (1, send_b, got_b, twin_b, back_b, out_b),
    ):

        @pl.loop(0, peers - 1)
        def _(i):
            peer = target(i)
            forth(step, send, got, peer, me).wait_send()
            home(step, back, out, peer, me).wait_send()

        @pl.loop(0, peers)
        def _(slot):
            across(step, got, other, slot).wait_send()

    for step, back, out in ((0, back_a, out_a), (1, back_b, out_b)):

        @pl.loop(0, peers - 1)
        def _(i):
            slot = source(i)
            home(step, back, out, slot, slot).wait_recv()


def fused(sizes):
    blks, lanes, own_heads = sizes
    peers = blks * lanes // 2
    span = own_heads * HEAD_DIM

    def run(qa, ka, va, qb, kb, vb, q_gain, k_gain):
        rows, width = qa.shape
        vmem = pl.BlockSpec(memory_space=pltpu.VMEM)
        block = jax.ShapeDtypeStruct((peers, rows, span), jnp.bfloat16)
        parts = pltpu.VMEM((peers, 3, rows, span), jnp.bfloat16)
        pairs = pltpu.VMEM((peers, 2, rows, span), jnp.bfloat16)
        whole = pltpu.VMEM((peers, rows, span), jnp.bfloat16)
        sem = pltpu.SemaphoreType.DMA((2, peers))
        outs = pl.pallas_call(
            functools.partial(fused_kernel, sizes),
            out_shape=(block, block),
            in_specs=[vmem] * 8,
            out_specs=(vmem, vmem),
            scratch_shapes=[parts] * 4 + [pairs] * 2 + [whole] * 2 + [sem] * 6,
            compiler_params=pltpu.CompilerParams(
                collective_id=0, has_side_effects=True, vmem_limit_bytes=40 * 1024 * 1024
            ),
        )(qa, ka, va, qb, kb, vb, q_gain.reshape(1, width), k_gain.reshape(1, width))
        return tuple(jnp.transpose(o, (1, 0, 2)).reshape(rows, width) for o in outs)

    return run


def solution(mesh):
    blks, lanes = mesh.shape["blk"], mesh.shape["head"]
    if lanes % 2 == 0 and HEADS % (blks * lanes // 2) == 0:
        body = fused((blks, lanes, HEADS // (blks * lanes // 2)))
    else:
        body = shards
    return jax.shard_map(
        body,
        mesh=mesh,
        in_specs=(
            P(("group", "blk", "head"), None),
            P(("group", "blk", "head"), None),
            P(("group", "blk", "head"), None),
            P(("group", "blk", "head"), None),
            P(("group", "blk", "head"), None),
            P(("group", "blk", "head"), None),
            P(),
            P(),
        ),
        out_specs=(P(("group", "blk", "head"), None), P(("group", "blk", "head"), None)),
        check_vma=False,
    )
```

```python
import functools
import math

import jax
import jax.numpy as jnp
from jax import lax
from jax.experimental import pallas as pl
from jax.experimental.pallas import tpu as pltpu
from jax.sharding import PartitionSpec as P

HEADS = 40
HEAD_DIM = 128


norm_eps = 1e-06


def normalize(values, gain_vec):
    widened = values.astype(jnp.float32)
    inverse = lax.rsqrt(jnp.mean(widened * widened, axis=-1, keepdims=True) + norm_eps)
    return (widened * inverse * gain_vec).astype(jnp.bfloat16)


def to_heads(matrix):
    return matrix.reshape(matrix.shape[0], HEADS, HEAD_DIM)


def binary_scale(magnitude):
    factor_now = jnp.full(magnitude.shape, 2.0 ** (-20), jnp.float32)
    for exponent in range(-20, 10):
        factor_now = factor_now * jnp.where(magnitude >= 2.0**exponent, 2.0, 1.0)
    return factor_now


def coarse_code(ratio):
    step_size = jnp.full(ratio.shape, 2.0 ** (-17), jnp.float32)
    magnitude = jnp.abs(ratio)
    for exponent in range(1, 15):
        step_size = step_size * jnp.where(magnitude >= 2.0 ** (-exponent), 2.0, 1.0)
    return jnp.floor(ratio / step_size + 0.5) * step_size


def block_length(total_rows):
    return max(
        (step_len for step_len in range(1, min(total_rows, 512) + 1) if total_rows % step_len == 0)
    )


def absorb(status, scores, value_rows, precise):
    run_max, run_sum, run_acc = status
    new_max = jnp.maximum(run_max, jnp.max(scores, axis=-1))
    factor = jnp.exp(run_max - new_max)
    weights = jnp.exp(scores - new_max[..., None])
    run_sum = run_sum * factor + jnp.sum(weights, axis=-1)
    if precise:
        update = jnp.einsum("qhk,khd->qhd", weights, value_rows, precision=lax.Precision.HIGHEST)
    else:
        update = jnp.einsum(
            "qhk,khd->qhd",
            weights.astype(jnp.bfloat16),
            value_rows,
            preferred_element_type=jnp.float32,
        )
    return (new_max, run_sum, run_acc * factor[..., None] + update)


def sweep(status, total_rows, block_fn):
    length = block_length(total_rows)

    def one_block(block_no, current):
        return block_fn(current, block_no * length, length)

    return lax.fori_loop(0, total_rows // length, one_block, status)


def rough_blocks(queries, key_rows, value_rows):
    inv_root = 1.0 / math.sqrt(queries.shape[-1])

    def block_fn(current, offset, length):
        key_blk = lax.dynamic_slice_in_dim(key_rows, offset, length, 0)
        value_blk = lax.dynamic_slice_in_dim(value_rows, offset, length, 0)
        scores = (
            jnp.einsum("qhd,khd->qhk", queries, key_blk, preferred_element_type=jnp.float32)
            * inv_root
        )
        return absorb(current, scores, value_blk, False)

    return block_fn


def exact_blocks(queries, cache_keys, cache_values, coded_rows, row_base):
    code_keys, code_values, scale_keys, scale_values = coded_rows
    inv_root = 1.0 / math.sqrt(queries.shape[-1])

    def block_fn(current, offset, length):
        old_keys = lax.dynamic_slice_in_dim(cache_keys, row_base + offset, length, 0).astype(
            jnp.float32
        )
        old_values = lax.dynamic_slice_in_dim(cache_values, row_base + offset, length, 0).astype(
            jnp.float32
        )
        key_scale = lax.dynamic_slice_in_dim(scale_keys, offset, length, 0).astype(jnp.float32)
        value_scale = lax.dynamic_slice_in_dim(scale_values, offset, length, 0).astype(jnp.float32)
        new_keys = old_keys + key_scale[..., None] * lax.dynamic_slice_in_dim(
            code_keys, offset, length, 0
        ).astype(jnp.float32)
        new_values = old_values + value_scale[..., None] * lax.dynamic_slice_in_dim(
            code_values, offset, length, 0
        ).astype(jnp.float32)
        scores = (
            jnp.einsum("qhd,khd->qhk", queries, new_keys, precision=lax.Precision.HIGHEST)
            * inv_root
        )
        return absorb(current, scores, new_values, True)

    return block_fn


def fresh_status(queries):
    leading = queries.shape[:2]
    return (
        jnp.full(leading, -jnp.inf, jnp.float32),
        jnp.zeros(leading, jnp.float32),
        jnp.zeros(queries.shape, jnp.float32),
    )


def finish(status):
    run_max, run_sum, run_acc = status
    return (run_acc / run_sum[..., None]).astype(jnp.bfloat16)


def send_back(result):
    moved = lax.all_to_all(result, "head", split_axis=0, concat_axis=1, tiled=True)
    return moved.reshape(moved.shape[0], moved.shape[1] * moved.shape[2])


def prepare(query, key_rows, value_rows, query_gain, key_gain):
    moved_query, moved_key, moved_value = (
        lax.all_to_all(
            to_heads(normalize(query, query_gain)), "head", split_axis=1, concat_axis=0, tiled=True
        ),
        lax.all_to_all(
            to_heads(normalize(key_rows, key_gain)), "head", split_axis=1, concat_axis=0, tiled=True
        ),
        lax.all_to_all(to_heads(value_rows), "head", split_axis=1, concat_axis=0, tiled=True),
    )
    return (moved_query, moved_key, moved_value)


def shards(query_a, key_a, value_a, query_b, key_b, value_b, query_gain, key_gain):
    queries_a, keys_a, values_a = prepare(query_a, key_a, value_a, query_gain, key_gain)
    queries_b, keys_b, values_b = prepare(query_b, key_b, value_b, query_gain, key_gain)
    total_rows = keys_a.shape[0] * lax.axis_size("blk")
    start_a = fresh_status(queries_a)
    cache_keys, cache_values = (
        lax.all_gather(keys_a, "blk", axis=0, tiled=True),
        lax.all_gather(values_a, "blk", axis=0, tiled=True),
    )
    status_a = sweep(start_a, total_rows, rough_blocks(queries_a, cache_keys, cache_values))
    attended_a = send_back(finish(status_a))
    residual_key = keys_b.astype(jnp.float32) - keys_a.astype(jnp.float32)
    residual_value = values_b.astype(jnp.float32) - values_a.astype(jnp.float32)
    scale_key = binary_scale(jnp.max(jnp.abs(residual_key), axis=-1)).astype(jnp.bfloat16)
    scale_value = binary_scale(jnp.max(jnp.abs(residual_value), axis=-1)).astype(jnp.bfloat16)
    code_key = coarse_code(residual_key / scale_key.astype(jnp.float32)[..., None]).astype(
        jnp.bfloat16
    )
    code_value = coarse_code(residual_value / scale_value.astype(jnp.float32)[..., None]).astype(
        jnp.bfloat16
    )
    queries_wide = queries_b.astype(jnp.float32)
    start_b = fresh_status(queries_b)
    gathered = (
        lax.all_gather(code_key, "blk", axis=0, tiled=True),
        lax.all_gather(code_value, "blk", axis=0, tiled=True),
        lax.all_gather(scale_key, "blk", axis=0, tiled=True),
        lax.all_gather(scale_value, "blk", axis=0, tiled=True),
    )
    status_b = sweep(
        start_b, total_rows, exact_blocks(queries_wide, cache_keys, cache_values, gathered, 0)
    )
    attended_b = send_back(finish(status_b))
    return (attended_a, attended_b)


MESH = pl.DeviceIdType.MESH


def stepped_code(ratio):
    magnitude = jnp.abs(ratio)
    step_size = jnp.full(ratio.shape, 2.0 ** (-17), jnp.float32)
    inverse = jnp.full(ratio.shape, 2.0**17, jnp.float32)
    for exponent in range(14, 0, -1):
        reached = magnitude >= 2.0 ** (-exponent)
        step_size = jnp.where(reached, 2.0 ** (-2 - exponent), step_size)
        inverse = jnp.where(reached, 2.0 ** (2 + exponent), inverse)
    return jnp.floor(ratio * inverse + 0.5) * step_size


def coded_residual(fresh, cached):
    residual = fresh - cached
    magnitude = jnp.max(jnp.abs(residual), axis=-1, keepdims=True)
    scale = jnp.full(magnitude.shape, 2.0 ** (-20), jnp.float32)
    inverse = jnp.full(magnitude.shape, 2.0**20, jnp.float32)
    for exponent in range(-20, 10):
        reached = magnitude >= 2.0**exponent
        scale = jnp.where(reached, 2.0 ** (exponent + 1), scale)
        inverse = jnp.where(reached, 2.0 ** (-exponent - 1), inverse)
    return stepped_code(residual * inverse) * scale


def fused_kernel(
    sizes, qa_far, ka_far, va_far, qb_far, kb_far, vb_far, q_gain_far, k_gain_far, out_a, out_b,
    qa, ka, va, qb, kb, vb, q_gain, k_gain, send_a, send_b, got_a, got_b, twin_a, twin_b, back_a, back_b,
    ssem, rsem, tsem, usem, osem, psem, isem, ksem,
):
    blks, lanes, own_heads = sizes
    half_lanes = lanes // 2
    peers = blks * half_lanes
    rows, width = qa.shape
    span = own_heads * HEAD_DIM
    blk, lane = lax.axis_index("blk"), lax.axis_index("head")
    side, core = lane // 2, lane % 2
    me = blk * half_lanes + side
    here = {"group": lax.axis_index("group")}

    def place(peer):
        return {**here, "blk": peer // half_lanes, "head": (peer % half_lanes) * 2 + core}

    twin = {**here, "blk": blk, "head": side * 2 + 1 - core}

    def target(i):
        return (me + i + 1) % peers

    def source(i):
        return (me + 2 * peers - 1 - i) % peers

    loads = [
        pltpu.make_async_copy(far, near, isem.at[n])
        for n, (far, near) in enumerate(
            (
                (qa_far, qa), (ka_far, ka), (q_gain_far, q_gain), (k_gain_far, k_gain),
                (va_far, va), (qb_far, qb), (kb_far, kb), (vb_far, vb),
            )
        )
    ]
    for load in loads:
        load.start()

    barrier = pltpu.get_barrier_semaphore()

    @pl.loop(0, peers - 1)
    def _(i):
        pl.semaphore_signal(barrier, inc=1, device_id=place(target(i)), device_id_type=MESH)

    pl.semaphore_signal(barrier, inc=1, device_id=twin, device_id_type=MESH)

    def columns(start):
        return pl.ds(pl.multiple_of(start, HEAD_DIM), HEAD_DIM)

    def inverse_norm(ref):
        def add(h, total):
            piece = ref[:, columns(h * HEAD_DIM)].astype(jnp.float32)
            return total + piece * piece

        total = lax.fori_loop(
            0, width // HEAD_DIM, add, jnp.zeros((rows, HEAD_DIM), jnp.float32), unroll=8
        )
        mean = jnp.sum(total, axis=-1, keepdims=True) * (1.0 / width)
        return lax.rsqrt(mean + norm_eps)

    for load in loads[:2]:
        load.wait()
    inv_qa, inv_ka = inverse_norm(qa), inverse_norm(ka)
    for load in loads[2:5]:
        load.wait()
    pl.semaphore_wait(barrier, peers)

    def normed(ref, inverse, gain, cols):
        piece = ref[:, cols].astype(jnp.float32)
        return (piece * inverse * gain[:, cols]).astype(jnp.bfloat16)

    def fill_a(dest, slot, peer):
        for h in range(own_heads):
            cols, local = columns(peer * span + h * HEAD_DIM), pl.ds(h * HEAD_DIM, HEAD_DIM)
            dest[slot, 0, :, local] = normed(qa, inv_qa, q_gain, cols)
            dest[slot, 1, :, local] = normed(ka, inv_ka, k_gain, cols)
            dest[slot, 2, :, local] = va[:, cols]

    def fill_b(dest, slot, peer):
        for h in range(own_heads):
            cols, local = columns(peer * span + h * HEAD_DIM), pl.ds(h * HEAD_DIM, HEAD_DIM)
            dest[slot, 0, :, local] = normed(qb, inv_qb, q_gain, cols)
            fresh = normed(kb, inv_kb, k_gain, cols).astype(jnp.float32)
            cached = normed(ka, inv_ka, k_gain, cols).astype(jnp.float32)
            dest[slot, 1, :, local] = coded_residual(fresh, cached).astype(jnp.bfloat16)
            dest[slot, 2, :, local] = coded_residual(
                vb[:, cols].astype(jnp.float32), va[:, cols].astype(jnp.float32)
            ).astype(jnp.bfloat16)

    def forth(step, send, got, peer, slot):
        return pltpu.make_async_remote_copy(
            src_ref=send.at[peer],
            dst_ref=got.at[slot],
            send_sem=ssem.at[step, peer],
            recv_sem=rsem.at[step, slot],
            device_id=place(peer),
            device_id_type=MESH,
        )

    def across(step, got, other, slot):
        return pltpu.make_async_remote_copy(
            src_ref=got.at[slot, pl.ds(1, 2)],
            dst_ref=other.at[slot],
            send_sem=tsem.at[step, slot],
            recv_sem=usem.at[step, slot],
            device_id=twin,
            device_id_type=MESH,
        )

    def home(step, back, out, peer, slot):
        return pltpu.make_async_remote_copy(
            src_ref=back.at[peer],
            dst_ref=out.at[:, pl.ds(pl.multiple_of(slot * span, HEAD_DIM), span)],
            send_sem=osem.at[step, peer],
            recv_sem=psem.at[step, slot],
            device_id=place(peer),
            device_id_type=MESH,
        )

    def keep(step, back, out):
        return pltpu.make_async_copy(
            back.at[me],
            out.at[:, pl.ds(pl.multiple_of(me * span, HEAD_DIM), span)],
            ksem.at[step],
        )

    @pl.loop(0, peers - 1)
    def _(i):
        peer = target(i)
        fill_a(send_a, peer, peer)
        forth(0, send_a, got_a, peer, me).start()

    fill_a(got_a, me, me)
    across(0, got_a, twin_a, me).start()

    for load in loads[5:]:
        load.wait()
    inv_qb, inv_kb = inverse_norm(qb), inverse_norm(kb)

    @pl.loop(0, peers - 1)
    def _(i):
        peer = target(i)
        fill_b(send_b, peer, peer)
        forth(1, send_b, got_b, peer, me).start()

    fill_b(got_b, me, me)
    across(1, got_b, twin_b, me).start()

    inv_root = 1.0 / math.sqrt(HEAD_DIM)

    def collect(step, send, got, other):
        @pl.loop(0, peers - 1)
        def _(i):
            slot = source(i)
            forth(step, send, got, slot, slot).wait_recv()
            across(step, got, other, slot).start()

        @pl.loop(0, peers)
        def _(slot):
            across(step, got, other, slot).wait_recv()

    def gather_rows(got, other, part, cols):
        own = got[:, part, :, cols].astype(jnp.float32).reshape(peers * rows, HEAD_DIM)
        far = other[:, part - 1, :, cols].astype(jnp.float32).reshape(peers * rows, HEAD_DIM)
        return jnp.concatenate([own, far], axis=0).astype(jnp.bfloat16)

    def query_rows(got, cols):
        own = got[:, 0, :, cols].astype(jnp.float32).reshape(peers * rows, HEAD_DIM)
        return own.astype(jnp.bfloat16)

    def scores_of(queries, keys):
        return (
            lax.dot_general(
                queries, keys, (((1,), (1,)), ((), ())), preferred_element_type=jnp.float32
            )
            * inv_root
        )

    def store_head(back, cols, result):
        back[:, :, cols] = result.reshape(peers, rows, HEAD_DIM).astype(jnp.bfloat16)

    collect(0, send_a, got_a, twin_a)

    @pl.loop(0, own_heads)
    def _(h):
        cols = columns(h * HEAD_DIM)
        scores = scores_of(query_rows(got_a, cols), gather_rows(got_a, twin_a, 1, cols))
        weights = jnp.exp(scores - jnp.max(scores, axis=1, keepdims=True))
        total = jnp.sum(weights, axis=1, keepdims=True)
        values = gather_rows(got_a, twin_a, 2, cols)
        mixed = jnp.dot(weights.astype(jnp.bfloat16), values, preferred_element_type=jnp.float32)
        store_head(back_a, cols, mixed / total)

    keep(0, back_a, out_a).start()
    @pl.loop(0, peers - 1)
    def _(i):
        home(0, back_a, out_a, target(i), me).start()

    collect(1, send_b, got_b, twin_b)

    @pl.loop(0, own_heads)
    def _(h):
        cols = columns(h * HEAD_DIM)
        queries = query_rows(got_b, cols)
        keys = jnp.concatenate(
            [gather_rows(got_a, twin_a, 1, cols), gather_rows(got_b, twin_b, 1, cols)], axis=1
        )
        scores = scores_of(jnp.concatenate([queries, queries], axis=1), keys)
        weights = jnp.exp(scores - jnp.max(scores, axis=1, keepdims=True))
        total = jnp.sum(weights, axis=1, keepdims=True)
        values = jnp.concatenate(
            [gather_rows(got_a, twin_a, 2, cols), gather_rows(got_b, twin_b, 2, cols)], axis=1
        )
        coarse = weights.astype(jnp.bfloat16)
        fine = (weights - coarse.astype(jnp.float32)).astype(jnp.bfloat16)
        mixed = jnp.dot(coarse, values, preferred_element_type=jnp.float32) + jnp.dot(
            fine, values, preferred_element_type=jnp.float32
        )
        store_head(back_b, cols, (mixed[:, :HEAD_DIM] + mixed[:, HEAD_DIM:]) / total)

    @pl.loop(0, peers - 1)
    def _(i):
        home(1, back_b, out_b, target(i), me).start()

    keep(1, back_b, out_b).start()

    for step, send, got, other, back, out in (
        (0, send_a, got_a, twin_a, back_a, out_a),
        (1, send_b, got_b, twin_b, back_b, out_b),
    ):

        @pl.loop(0, peers - 1)
        def _(i):
            peer = target(i)
            forth(step, send, got, peer, me).wait_send()
            home(step, back, out, peer, me).wait_send()

        @pl.loop(0, peers)
        def _(slot):
            across(step, got, other, slot).wait_send()

    for step, back, out in ((0, back_a, out_a), (1, back_b, out_b)):

        @pl.loop(0, peers - 1)
        def _(i):
            slot = source(i)
            home(step, back, out, slot, slot).wait_recv()

        keep(step, back, out).wait()


def fused(sizes):
    blks, lanes, own_heads = sizes
    peers = blks * lanes // 2
    span = own_heads * HEAD_DIM

    def run(qa, ka, va, qb, kb, vb, q_gain, k_gain):
        rows, width = qa.shape
        far = pl.BlockSpec(memory_space=pl.ANY)
        block = jax.ShapeDtypeStruct((rows, width), jnp.bfloat16)
        parts = pltpu.VMEM((peers, 3, rows, span), jnp.bfloat16)
        pairs = pltpu.VMEM((peers, 2, rows, span), jnp.bfloat16)
        whole = pltpu.VMEM((peers, rows, span), jnp.bfloat16)
        sem = pltpu.SemaphoreType.DMA((2, peers))
        outs = pl.pallas_call(
            functools.partial(fused_kernel, sizes),
            out_shape=(block, block),
            in_specs=[far] * 8,
            out_specs=(far, far),
            scratch_shapes=[pltpu.VMEM((rows, width), jnp.bfloat16)] * 6
            + [pltpu.VMEM((1, width), jnp.float32)] * 2
            + [parts] * 4 + [pairs] * 2 + [whole] * 2 + [sem] * 6
            + [pltpu.SemaphoreType.DMA((8,)), pltpu.SemaphoreType.DMA((2,))],
            compiler_params=pltpu.CompilerParams(
                collective_id=0, has_side_effects=True, vmem_limit_bytes=56 * 1024 * 1024
            ),
        )(qa, ka, va, qb, kb, vb, q_gain.reshape(1, width), k_gain.reshape(1, width))
        return tuple(outs)

    return run


def solution(mesh):
    blks, lanes = mesh.shape["blk"], mesh.shape["head"]
    if lanes % 2 == 0 and HEADS % (blks * lanes // 2) == 0:
        body = fused((blks, lanes, HEADS // (blks * lanes // 2)))
    else:
        body = shards
    return jax.shard_map(
        body,
        mesh=mesh,
        in_specs=(
            P(("group", "blk", "head"), None),
            P(("group", "blk", "head"), None),
            P(("group", "blk", "head"), None),
            P(("group", "blk", "head"), None),
            P(("group", "blk", "head"), None),
            P(("group", "blk", "head"), None),
            P(),
            P(),
        ),
        out_specs=(P(("group", "blk", "head"), None), P(("group", "blk", "head"), None)),
        check_vma=False,
    )
```
